1024 devices in a mesh: section: 16 (over z), row: 16 (over y, core), col: 4 (over x).
Axes of the slice: x: 4, y: 8, z: 16, core: 2. Of those that a mesh axis runs over, the one named last changes fastest.
Arguments:
- tokens: bfloat16 [16, 512, 3072], P('section', None, 'col'), may hold values from -6 to 6
- up_weight: bfloat16 [16, 3072, 12288], P('section', 'col', 'row'), may hold values from -0.109375 to 0.109375
- down_weight: bfloat16 [16, 12288, 3072], P('section', 'row', 'col'), may hold values from -0.0546875 to 0.0546875
- out_grad: bfloat16 [16, 512, 3072], P('section', None, 'col'), may hold values from -6 to 6
- saved_hidden: bfloat16 [16, 512, 12288], P('section', 'col', 'row'), may hold values from -6 to 6
Outputs:
- next_tokens: bfloat16 [16, 512, 3072], P('section', None, 'col')
- prev_grads: bfloat16 [16, 512, 3072], P('section', None, 'col')
The draws below stay inside these ranges and needn't reach their ends.
All inputs are finite; a program needn't handle non-finite values.
Results may differ from the reference program's by a relative error of at most 0.019.
Values may be sent and summed in bfloat16 or wider, within the bound.
No kernel may reach another device: no remote copies, remote signals or barrier semaphores. Data moves between devices by JAX's collectives and lax.ppermute only.
A program may use at most 32 MiB of HBM per device.

```python
import jax
import jax.numpy as jnp
from jax import lax

D = 3072
F = 12288
TOKENS = 512
SECTIONS = 16
BLOCKS = 16
HID_BLOCK = 768


def level_of(rng, extent, cuts, smallest, high):
    def one(dim, shards_of):
        heights = jax.random.uniform(jax.random.fold_in(jax.random.fold_in(rng, 6), dim), (shards_of,), jnp.float32, smallest / len(cuts), high / len(cuts))
        return jnp.repeat(jnp.exp(heights), extent[dim] // shards_of).reshape((-1,) + (1,) * (len(extent) - dim - 1))

    loudness = one(*cuts[0])
    for cut in cuts[1:]:
        loudness = loudness * one(*cut)
    return loudness


def gaussian(rng, dims, scale, reach, split=(), kind=jnp.bfloat16):
    factor_of = level_of(rng, dims, split, -0.22, 0.18) if split else 1.0
    entries = jax.random.normal(rng, dims, jnp.float32) * scale * factor_of
    return jnp.minimum(jnp.maximum(entries, -reach), reach).astype(kind)


def setup_inputs(seed: int = 0) -> dict:
    arg_keys = jax.random.split(jax.random.key(seed), 6)
    return {
        "tokens": gaussian(arg_keys[0], (SECTIONS, TOKENS, D), 1.0, 6.0, ((0, 16), (2, 4))),
        "up_weight": gaussian(arg_keys[1], (SECTIONS, D, F), D ** -0.5, 0.109375, ((0, 16), (1, 4), (2, 16))),
        "down_weight": gaussian(arg_keys[2], (SECTIONS, F, D), F ** -0.5, 0.0546875, ((0, 16), (1, 16), (2, 4))),
        "out_grad": gaussian(arg_keys[3], (SECTIONS, TOKENS, D), 1.0, 6.0, ((0, 16), (2, 4))),
        "saved_hidden": gaussian(arg_keys[4], (SECTIONS, TOKENS, F), 1.0, 6.0, ((0, 16), (1, 4), (2, 16))),
    }


inv_root_two = 0.7071067811865476
inv_root_tau = 0.3989422804014327


def gelu_value(hidden):
    return 0.5 * hidden * (1.0 + lax.erf(hidden * inv_root_two))


def gelu_slope(hidden):
    return 0.5 * (1.0 + lax.erf(hidden * inv_root_two)) + hidden * jnp.exp(-0.5 * hidden * hidden) * inv_root_tau


def blockwise(operand, weight_blocks, contract):
    operand_blocks = operand.reshape(operand.shape[0], BLOCKS, HID_BLOCK).transpose(1, 0, 2)

    def add_block(carry, pair):
        product = lax.dot_general(pair[0], pair[1], (((1,), (contract,)), ((), ())), preferred_element_type=jnp.float32)
        rounded = lax.optimization_barrier(product.astype(jnp.bfloat16))
        return carry + rounded.astype(jnp.float32), None

    initial = jnp.zeros((operand.shape[0], D), jnp.float32)
    summed, _ = lax.scan(add_block, initial, (operand_blocks, weight_blocks))
    return summed


def one_section(packed):
    inputs, w_up, w_down, upstream, stored = packed
    hidden = jnp.dot(inputs, w_up, preferred_element_type=jnp.float32)
    active = gelu_value(hidden).astype(jnp.bfloat16)
    forward_sum = blockwise(active, w_down.reshape(BLOCKS, HID_BLOCK, D), 0)
    output = (inputs.astype(jnp.float32) + forward_sum).astype(jnp.bfloat16)
    slope_in = lax.dot_general(upstream, w_down, (((1,), (1,)), ((), ())), preferred_element_type=jnp.float32)
    hidden_grad = (slope_in * gelu_slope(stored.astype(jnp.float32))).astype(jnp.bfloat16)
    up_blocks = w_up.reshape(D, BLOCKS, HID_BLOCK).transpose(1, 0, 2)
    back_sum = blockwise(hidden_grad, up_blocks, 1)
    grad_in = (upstream.astype(jnp.float32) + back_sum).astype(jnp.bfloat16)
    return output, grad_in


def reference(tokens, up_weight, down_weight, out_grad, saved_hidden):
    outputs, grads = lax.map(one_section, (tokens, up_weight, down_weight, out_grad, saved_hidden))
    return jnp.roll(outputs, 1, axis=0), jnp.roll(grads, -1, axis=0)
```

```python
import jax
import jax.numpy as jnp
from jax import lax
from jax.sharding import Mesh, PartitionSpec as P

inv_root_two = 0.7071067811865476
inv_root_tau = 0.3989422804014327


def passed_along(block, axis, distance):
    devices = range(lax.axis_size(axis))
    route = [((i - distance) % len(devices), i) for i in devices]
    return lax.ppermute(block, axis, route)


def gelu_value(hidden):
    return 0.5 * hidden * (1.0 + lax.erf(hidden * inv_root_two))


def gelu_slope(hidden):
    return (
        0.5 * (1.0 + lax.erf(hidden * inv_root_two))
        + hidden * jnp.exp(-0.5 * hidden * hidden) * inv_root_tau
    )


def product(operand, weight, contract):
    return lax.dot_general(
        operand, weight, (((1,), (contract,)), ((), ())), preferred_element_type=jnp.float32
    )


def hidden_share(operand, weight, contract):
    n = lax.axis_size("col")
    partial = product(operand, weight, contract).astype(jnp.bfloat16)
    parts = lax.all_to_all(partial.reshape(n, -1, partial.shape[1]), "col", 0, 0, tiled=True)
    return parts.astype(jnp.float32).sum(0)


def feature_sum(hidden_part, weight, contract, residual, shift_by):
    rows, ny = lax.axis_size("y") * lax.axis_size("core"), lax.axis_size("y")
    gathered = lax.all_gather(hidden_part, "col", axis=0, tiled=True)
    tokens, width = gathered.shape
    piece = tokens // rows
    by_core = gathered.reshape(ny, 2, piece, width)
    core = lax.axis_index("core")
    theirs = lax.dynamic_slice_in_dim(by_core, 1 - core, 1, 1).reshape(tokens // 2, width)
    ours = lax.dynamic_slice_in_dim(by_core, core, 1, 1).reshape(tokens // 2, width)
    sent = product(theirs, weight, contract).astype(jnp.bfloat16)
    arrived = passed_along(sent, "core", 1)
    chip_sum = (product(ours, weight, contract) + arrived.astype(jnp.float32)).astype(jnp.bfloat16)
    parts = lax.all_to_all(chip_sum.reshape(ny, piece, -1), "y", 0, 0, tiled=True)
    summed = parts.astype(jnp.float32).sum(0)
    mine = lax.axis_index("y") * 2 + core
    own_residual = lax.dynamic_slice_in_dim(residual, mine * piece, piece, 0)
    result = (own_residual.astype(jnp.float32) + summed).astype(jnp.bfloat16)
    moved = passed_along(result, "section", shift_by)
    return lax.all_gather(moved, ("y", "core"), axis=0, tiled=True)


def body(tokens, up_weight, down_weight, out_grad, saved_hidden):
    inputs = tokens[0]
    w_up = up_weight[0]
    w_down = down_weight[0]
    upstream = out_grad[0]
    stored = saved_hidden[0].astype(jnp.float32)
    hidden = hidden_share(inputs, w_up, 0)
    active = gelu_value(hidden).astype(jnp.bfloat16)
    next_tokens = feature_sum(active, w_down, 0, inputs, 1)
    slope_in = hidden_share(upstream, w_down, 1)
    hidden_grad = (slope_in * gelu_slope(stored)).astype(jnp.bfloat16)
    prev_grads = feature_sum(hidden_grad, w_up, 1, upstream, -1)
    return (next_tokens[None], prev_grads[None])


def solution(mesh):
    sections, rows, cols = mesh.devices.shape
    fine = Mesh(mesh.devices.reshape(sections, rows // 2, 2, cols), ("section", "y", "core", "col"))
    features = P("section", None, "col")
    return jax.shard_map(
        body,
        mesh=fine,
        in_specs=(
            features,
            P("section", "col", ("y", "core")),
            P("section", ("y", "core"), "col"),
            features,
            P("section", "col", ("y", "core")),
        ),
        out_specs=(features, features),
        check_vma=False,
    )
```

```python
import jax
import jax.numpy as jnp
from jax import lax
from jax.sharding import Mesh, PartitionSpec as P

inv_root_two = 0.7071067811865476
inv_root_tau = 0.3989422804014327


def passed_along(block, axis, distance):
    devices = range(lax.axis_size(axis))
    route = [((i - distance) % len(devices), i) for i in devices]
    return lax.ppermute(block, axis, route)


def gelu_value(hidden):
    return 0.5 * hidden * (1.0 + lax.erf(hidden * inv_root_two))


def gelu_slope(hidden):
    return (
        0.5 * (1.0 + lax.erf(hidden * inv_root_two))
        + hidden * jnp.exp(-0.5 * hidden * hidden) * inv_root_tau
    )


def product(operand, weight, contract):
    return lax.dot_general(
        operand, weight, (((1,), (contract,)), ((), ())), preferred_element_type=jnp.float32
    )


def hidden_share(operand, weight, contract):
    n = lax.axis_size("col")
    partial = product(operand, weight, contract).astype(jnp.bfloat16)
    parts = lax.all_to_all(partial.reshape(n, -1, partial.shape[1]), "col", 0, 0, tiled=True)
    return parts.astype(jnp.float32).sum(0)


def given_to_all(block, axis):
    copies = jnp.broadcast_to(block[None], (lax.axis_size(axis),) + block.shape)
    blocks = lax.all_to_all(copies, axis, 0, 0, tiled=True)
    return blocks.reshape(-1, block.shape[1])


def feature_sum(hidden_part, weight, contract, residual, shift_by):
    ny = lax.axis_size("y")
    gathered = given_to_all(hidden_part, "col")
    half = gathered.shape[0] // 2
    piece = half // ny
    core = lax.axis_index("core")
    theirs = lax.dynamic_slice_in_dim(gathered, (1 - core) * half, half, 0)
    ours = lax.dynamic_slice_in_dim(gathered, core * half, half, 0)
    sent = product(theirs, weight, contract).astype(jnp.bfloat16)
    arrived = passed_along(sent, "core", 1)
    chip_sum = (product(ours, weight, contract) + arrived.astype(jnp.float32)).astype(jnp.bfloat16)
    parts = lax.all_to_all(chip_sum.reshape(ny, piece, -1), "y", 0, 0, tiled=True)
    summed = parts.astype(jnp.float32).sum(0)
    mine = core * ny + lax.axis_index("y")
    own_residual = lax.dynamic_slice_in_dim(residual, mine * piece, piece, 0)
    result = (own_residual.astype(jnp.float32) + summed).astype(jnp.bfloat16)
    moved = passed_along(result, "section", shift_by)
    return lax.all_gather(given_to_all(moved, "y"), "core", axis=0, tiled=True)


def body(tokens, up_weight, down_weight, out_grad, saved_hidden):
    inputs = tokens[0]
    w_up = up_weight[0]
    w_down = down_weight[0]
    upstream = out_grad[0]
    stored = saved_hidden[0].astype(jnp.float32)
    hidden = hidden_share(inputs, w_up, 0)
    active = gelu_value(hidden).astype(jnp.bfloat16)
    next_tokens = feature_sum(active, w_down, 0, inputs, 1)
    slope_in = hidden_share(upstream, w_down, 1)
    hidden_grad = (slope_in * gelu_slope(stored)).astype(jnp.bfloat16)
    prev_grads = feature_sum(hidden_grad, w_up, 1, upstream, -1)
    return (next_tokens[None], prev_grads[None])


def solution(mesh):
    sections, rows, cols = mesh.devices.shape
    fine = Mesh(mesh.devices.reshape(sections, rows // 2, 2, cols), ("section", "y", "core", "col"))
    features = P("section", None, "col")
    return jax.shard_map(
        body,
        mesh=fine,
        in_specs=(
            features,
            P("section", "col", ("y", "core")),
            P("section", ("y", "core"), "col"),
            features,
            P("section", "col", ("y", "core")),
        ),
        out_specs=(features, features),
        check_vma=False,
    )
```

```python
import jax
import jax.numpy as jnp
from jax import lax
from jax.sharding import Mesh, PartitionSpec as P

inv_root_two = 0.7071067811865476
inv_root_tau = 0.3989422804014327


def gelu_value(hidden):
    return 0.5 * hidden * (1.0 + lax.erf(hidden * inv_root_two))


def gelu_slope(hidden):
    return (
        0.5 * (1.0 + lax.erf(hidden * inv_root_two))
        + hidden * jnp.exp(-0.5 * hidden * hidden) * inv_root_tau
    )


def product(operand, weight, contract):
    return lax.dot_general(
        operand, weight, (((1,), (contract,)), ((), ())), preferred_element_type=jnp.float32
    )


def swapped(block):
    return lax.ppermute(block, "core", [(0, 1), (1, 0)])


def body(tokens, up_weight, down_weight, out_grad, saved_hidden):
    inputs, w_up, w_down, upstream = tokens[0], up_weight[0], down_weight[0], out_grad[0]
    stored = saved_hidden[0].astype(jnp.float32)
    ncol, ny, nz = lax.axis_size("col"), lax.axis_size("y"), lax.axis_size("section")
    core = lax.axis_index("core")
    forward = core == 0
    count = inputs.shape[0]
    arrived = swapped(jnp.where(forward, w_up, w_down))

    def by_col(partial):
        return partial.astype(jnp.bfloat16).reshape(ncol, count // ncol, -1)

    partials = jnp.stack(
        [by_col(product(inputs, w_up, 0)), by_col(product(upstream, w_down, 1))], axis=1
    )
    sums = lax.all_to_all(partials, "col", 0, 0, tiled=True).astype(jnp.float32).sum(0)
    active = gelu_value(sums[0]).astype(jnp.bfloat16)
    hidden_grad = (sums[1] * gelu_slope(stored)).astype(jnp.bfloat16)
    copies = jnp.concatenate(
        [jnp.broadcast_to(part[None], (ncol,) + part.shape) for part in (active, hidden_grad)]
    )
    gathered = lax.all_to_all(copies, ("core", "col"), 0, 0, tiled=True)
    first = gathered[:ncol].reshape(count, -1)
    second = gathered[ncol:].reshape(count, -1)
    chip_sum = lax.cond(
        forward,
        lambda: product(first, w_down, 0) + product(second, arrived, 0),
        lambda: product(first, arrived, 1) + product(second, w_up, 1),
    ).astype(jnp.bfloat16)
    piece = count // ny
    summed = lax.all_to_all(chip_sum.reshape(ny, piece, -1), "y", 0, 0, tiled=True)
    summed = summed.astype(jnp.float32).sum(0)
    start = lax.axis_index("y") * piece
    residual = jnp.where(
        forward,
        lax.dynamic_slice_in_dim(inputs, start, piece, 0),
        lax.dynamic_slice_in_dim(upstream, start, piece, 0),
    )
    result = (residual.astype(jnp.float32) + summed).astype(jnp.bfloat16)
    route = [(2 * s, 2 * ((s + 1) % nz)) for s in range(nz)]
    route += [(2 * s + 1, 2 * ((s - 1) % nz) + 1) for s in range(nz)]
    moved = lax.ppermute(result, ("section", "core"), route)
    pieces = jnp.broadcast_to(moved[None], (ny,) + moved.shape)
    mine = lax.all_to_all(pieces, "y", 0, 0, tiled=True).reshape(count, -1)
    other = swapped(mine)
    next_tokens = jnp.where(forward, mine, other)
    prev_grads = jnp.where(forward, other, mine)
    return (next_tokens[None], prev_grads[None])


def solution(mesh):
    sections, rows, cols = mesh.devices.shape
    fine = Mesh(mesh.devices.reshape(sections, rows // 2, 2, cols), ("section", "y", "core", "col"))
    features = P("section", None, "col")
    return jax.shard_map(
        body,
        mesh=fine,
        in_specs=(
            features,
            P("section", "col", ("y", "core")),
            P("section", ("y", "core"), "col"),
            features,
            P("section", "col", ("y", "core")),
        ),
        out_specs=(features, features),
        check_vma=False,
    )
```

```python
import jax
import jax.numpy as jnp
from jax import lax
from jax.experimental import pallas as pl
from jax.experimental.pallas import tpu as pltpu
from jax.sharding import Mesh, PartitionSpec as P

inv_root_two = 0.7071067811865476
inv_root_tau = 0.3989422804014327


def gelu_value(hidden):
    return 0.5 * hidden * (1.0 + lax.erf(hidden * inv_root_two))


def gelu_slope(hidden):
    return (
        0.5 * (1.0 + lax.erf(hidden * inv_root_two))
        + hidden * jnp.exp(-0.5 * hidden * hidden) * inv_root_tau
    )


def product(operand, weight, contract):
    return lax.dot_general(
        operand, weight, (((1,), (contract,)), ((), ())), preferred_element_type=jnp.float32
    )


def swapped(block):
    return lax.ppermute(block, "core", [(0, 1), (1, 0)])


def hidden_kernel(parts_ref, stored_ref, copies_ref):
    ncol = parts_ref.shape[0]
    sums = parts_ref[0].astype(jnp.float32)
    for i in range(1, ncol):
        sums += parts_ref[i].astype(jnp.float32)
    active = gelu_value(sums[0]).astype(jnp.bfloat16)
    hidden_grad = (sums[1] * gelu_slope(stored_ref[...].astype(jnp.float32))).astype(jnp.bfloat16)
    for i in range(ncol):
        copies_ref[0, i] = active
        copies_ref[1, i] = hidden_grad


def hidden_copies(parts, stored, steps=2):
    ncol, _, rows, width = parts.shape
    tile = rows // steps
    return pl.pallas_call(
        hidden_kernel,
        grid=(steps,),
        in_specs=[
            pl.BlockSpec((ncol, 2, tile, width), lambda i: (0, 0, i, 0)),
            pl.BlockSpec((tile, width), lambda i: (i, 0)),
        ],
        out_specs=pl.BlockSpec((2, ncol, tile, width), lambda i: (0, 0, i, 0)),
        out_shape=jax.ShapeDtypeStruct((2, ncol, rows, width), jnp.bfloat16),
        compiler_params=pltpu.CompilerParams(vmem_limit_bytes=32 << 20),
    )(parts, stored)


def feature_kernel(core_ref, hidden_ref, own_ref, arrived_ref, out_ref):
    def both(first_weight, second_weight, contract):
        total = product(hidden_ref[0], first_weight[...], contract)
        total += product(hidden_ref[1], second_weight[...], contract)
        out_ref[...] = total.astype(jnp.bfloat16)

    @pl.when(core_ref[0] == 0)
    def _():
        both(own_ref, arrived_ref, 0)

    @pl.when(core_ref[0] != 0)
    def _():
        both(arrived_ref, own_ref, 1)


def feature_terms(core, hidden, own, arrived, steps=2):
    _, rows, width = hidden.shape
    tile = rows // steps
    whole = pl.BlockSpec(own.shape, lambda i, core: (0, 0))
    return pl.pallas_call(
        feature_kernel,
        grid_spec=pltpu.PrefetchScalarGridSpec(
            num_scalar_prefetch=1,
            grid=(steps,),
            in_specs=[
                pl.BlockSpec((2, tile, width), lambda i, core: (0, i, 0)),
                whole,
                whole,
            ],
            out_specs=pl.BlockSpec((tile, width), lambda i, core: (i, 0)),
        ),
        out_shape=jax.ShapeDtypeStruct((rows, own.shape[0]), jnp.bfloat16),
        compiler_params=pltpu.CompilerParams(vmem_limit_bytes=32 << 20),
    )(core.reshape(1), hidden, own, arrived)


def body(tokens, up_weight, down_weight, out_grad, saved_hidden):
    inputs, w_up, w_down, upstream = tokens[0], up_weight[0], down_weight[0], out_grad[0]
    ncol, ny, nz = lax.axis_size("col"), lax.axis_size("y"), lax.axis_size("section")
    core = lax.axis_index("core")
    forward = core == 0
    count = inputs.shape[0]

    def by_col(partial):
        return partial.astype(jnp.bfloat16).reshape(ncol, count // ncol, -1)

    partials = jnp.stack(
        [by_col(product(inputs, w_up, 0)), by_col(product(upstream, w_down, 1))], axis=1
    )
    piece = count // ny
    start = lax.axis_index("y") * piece
    partials, core, forward, start = lax.optimization_barrier((partials, core, forward, start))
    parts = lax.all_to_all(partials, "col", 0, 0, tiled=True)
    own = jnp.where(forward, w_down, w_up)
    arrived = swapped(jnp.where(forward, w_up, w_down))
    copies = hidden_copies(parts, saved_hidden[0])
    copies = copies.reshape((2 * ncol,) + copies.shape[2:])
    gathered = lax.all_to_all(copies, ("core", "col"), 0, 0, tiled=True)
    chip_sum = feature_terms(core, gathered.reshape(2, count, -1), own, arrived)
    residual = jnp.where(
        forward,
        lax.dynamic_slice_in_dim(inputs, start, piece, 0),
        lax.dynamic_slice_in_dim(upstream, start, piece, 0),
    )
    chip_sum, residual = lax.optimization_barrier((chip_sum, residual))
    summed = lax.all_to_all(chip_sum.reshape(ny, piece, -1), "y", 0, 0, tiled=True)
    summed = summed.astype(jnp.float32).sum(0)
    result = (residual.astype(jnp.float32) + summed).astype(jnp.bfloat16)
    route = [(2 * s, 2 * ((s + 1) % nz)) for s in range(nz)]
    route += [(2 * s + 1, 2 * ((s - 1) % nz) + 1) for s in range(nz)]
    moved = lax.ppermute(result, ("section", "core"), route)
    pieces = jnp.broadcast_to(moved[None], (ny,) + moved.shape)
    mine = lax.all_to_all(pieces, "y", 0, 0, tiled=True).reshape(count, -1)
    other = swapped(mine)
    next_tokens = jnp.where(forward, mine, other)
    prev_grads = jnp.where(forward, other, mine)
    return (next_tokens[None], prev_grads[None])


def solution(mesh):
    sections, rows, cols = mesh.devices.shape
    fine = Mesh(mesh.devices.reshape(sections, rows // 2, 2, cols), ("section", "y", "core", "col"))
    features = P("section", None, "col")
    return jax.shard_map(
        body,
        mesh=fine,
        in_specs=(
            features,
            P("section", "col", ("y", "core")),
            P("section", ("y", "core"), "col"),
            features,
            P("section", "col", ("y", "core")),
        ),
        out_specs=(features, features),
        check_vma=False,
    )
```

```python
import jax
import jax.numpy as jnp
from jax import lax
from jax.experimental import pallas as pl
from jax.experimental.pallas import tpu as pltpu
from jax.sharding import Mesh, PartitionSpec as P

inv_root_two = 0.7071067811865476
inv_root_tau = 0.3989422804014327


def gelu_value(hidden):
    return 0.5 * hidden * (1.0 + lax.erf(hidden * inv_root_two))


def gelu_slope(hidden):
    return (
        0.5 * (1.0 + lax.erf(hidden * inv_root_two))
        + hidden * jnp.exp(-0.5 * hidden * hidden) * inv_root_tau
    )


def product(operand, weight, contract):
    return lax.dot_general(
        operand, weight, (((1,), (contract,)), ((), ())), preferred_element_type=jnp.float32
    )


def swapped(block):
    return lax.ppermute(block, "core", [(0, 1), (1, 0)])


def partial_kernel(chunks_ref, inputs_ref, upstream_ref, up_ref, down_ref, *out_refs):
    terms = [
        product(inputs_ref[...], up_ref[...], 0).astype(jnp.bfloat16),
        product(upstream_ref[...], down_ref[...], 1).astype(jnp.bfloat16),
    ]
    for step, out_ref in enumerate(out_refs):

        @pl.when(pl.program_id(0) == step)
        def _():
            out_ref[0], out_ref[1] = terms


def partial_sums(chunks, count, inputs, upstream, w_up, w_down, rows):
    width = w_up.shape[1]
    chunk = pl.BlockSpec((rows, inputs.shape[1]), lambda i, chunks: (chunks[i], 0))
    whole = pl.BlockSpec(w_up.shape, lambda i, chunks: (0, 0))
    kept = pl.BlockSpec((2, rows, width), lambda i, chunks: (0, 0, 0))
    return pl.pallas_call(
        partial_kernel,
        grid_spec=pltpu.PrefetchScalarGridSpec(
            num_scalar_prefetch=1,
            grid=(count,),
            in_specs=[chunk, chunk, whole, whole],
            out_specs=[kept] * count,
        ),
        out_shape=[jax.ShapeDtypeStruct((2, rows, width), jnp.bfloat16)] * count,
        compiler_params=pltpu.CompilerParams(vmem_limit_bytes=58 << 20),
    )(chunks, inputs, upstream, w_up, w_down)


def hidden_kernel(*refs):
    *part_refs, stored_ref, copies_ref = refs
    sums = sum(part_ref[...].astype(jnp.float32) for part_ref in part_refs)
    active = gelu_value(sums[0]).astype(jnp.bfloat16)
    hidden_grad = (sums[1] * gelu_slope(stored_ref[...].astype(jnp.float32))).astype(jnp.bfloat16)
    for i in range(copies_ref.shape[1]):
        copies_ref[0, i] = active
        copies_ref[1, i] = hidden_grad


def hidden_copies(parts, stored, steps=2):
    _, rows, width = parts[0].shape
    tile = rows // steps
    return pl.pallas_call(
        hidden_kernel,
        grid=(steps,),
        in_specs=[pl.BlockSpec((2, tile, width), lambda i: (0, i, 0))] * len(parts)
        + [pl.BlockSpec((tile, width), lambda i: (i, 0))],
        out_specs=pl.BlockSpec((2, len(parts), tile, width), lambda i: (0, 0, i, 0)),
        out_shape=jax.ShapeDtypeStruct((2, len(parts), rows, width), jnp.bfloat16),
        compiler_params=pltpu.CompilerParams(vmem_limit_bytes=32 << 20),
    )(*parts, stored)


def feature_kernel(core_ref, hidden_ref, own_ref, arrived_ref, out_ref):
    def both(first_weight, second_weight, contract):
        total = product(hidden_ref[0], first_weight[...], contract)
        total += product(hidden_ref[1], second_weight[...], contract)
        out_ref[...] = total.astype(jnp.bfloat16)

    @pl.when(core_ref[0] == 0)
    def _():
        both(own_ref, arrived_ref, 0)

    @pl.when(core_ref[0] != 0)
    def _():
        both(arrived_ref, own_ref, 1)


def feature_terms(core, hidden, own, arrived, steps=2):
    _, rows, width = hidden.shape
    tile = rows // steps
    whole = pl.BlockSpec(own.shape, lambda i, core: (0, 0))
    return pl.pallas_call(
        feature_kernel,
        grid_spec=pltpu.PrefetchScalarGridSpec(
            num_scalar_prefetch=1,
            grid=(steps,),
            in_specs=[
                pl.BlockSpec((2, tile, width), lambda i, core: (0, i, 0)),
                whole,
                whole,
            ],
            out_specs=pl.BlockSpec((tile, width), lambda i, core: (i, 0)),
        ),
        out_shape=jax.ShapeDtypeStruct((rows, own.shape[0]), jnp.bfloat16),
        compiler_params=pltpu.CompilerParams(vmem_limit_bytes=32 << 20),
    )(core.reshape(1), hidden, own, arrived)


def body(tokens, up_weight, down_weight, out_grad, saved_hidden):
    inputs, w_up, w_down, upstream = tokens[0], up_weight[0], down_weight[0], out_grad[0]
    ncol, ny, nz = lax.axis_size("col"), lax.axis_size("y"), lax.axis_size("section")
    core = lax.axis_index("core")
    forward = core == 0
    count = inputs.shape[0]
    piece = count // ny
    start = lax.axis_index("y") * piece
    col = lax.axis_index("col")
    operands = (inputs, upstream, w_up, w_down, count // ncol)
    reach = sorted(range(1, ncol), key=lambda d: -min(d, ncol - d))
    chunks = jnp.stack([(col + d) % ncol for d in reach] + [col])
    terms = partial_sums(chunks, ncol, *operands)
    parts = [terms[-1]] + [
        lax.ppermute(term, "col", [(i, (i + d) % ncol) for i in range(ncol)])
        for d, term in zip(reach, terms)
    ]
    copies = hidden_copies(parts, saved_hidden[0])
    copies = copies.reshape((2 * ncol,) + copies.shape[2:])
    copies, w_up, w_down = lax.optimization_barrier((copies, w_up, w_down))
    own = jnp.where(forward, w_down, w_up)
    arrived = swapped(jnp.where(forward, w_up, w_down))
    residual = jnp.where(
        forward,
        lax.dynamic_slice_in_dim(inputs, start, piece, 0),
        lax.dynamic_slice_in_dim(upstream, start, piece, 0),
    )
    gathered = lax.all_to_all(copies, ("core", "col"), 0, 0, tiled=True)
    chip_sum = feature_terms(core, gathered.reshape(2, count, -1), own, arrived)
    chip_sum, residual = lax.optimization_barrier((chip_sum, residual))
    summed = lax.all_to_all(chip_sum.reshape(ny, piece, -1), "y", 0, 0, tiled=True)
    summed = summed.astype(jnp.float32).sum(0)
    result = (residual.astype(jnp.float32) + summed).astype(jnp.bfloat16)
    route = [(2 * s, 2 * ((s + 1) % nz)) for s in range(nz)]
    route += [(2 * s + 1, 2 * ((s - 1) % nz) + 1) for s in range(nz)]
    moved = lax.ppermute(result, ("section", "core"), route)
    pieces = jnp.broadcast_to(moved[None], (ny,) + moved.shape)
    mine = lax.all_to_all(pieces, "y", 0, 0, tiled=True).reshape(count, -1)
    other = swapped(mine)
    next_tokens = jnp.where(forward, mine, other)
    prev_grads = jnp.where(forward, other, mine)
    return (next_tokens[None], prev_grads[None])


def solution(mesh):
    sections, rows, cols = mesh.devices.shape
    fine = Mesh(mesh.devices.reshape(sections, rows // 2, 2, cols), ("section", "y", "core", "col"))
    features = P("section", None, "col")
    return jax.shard_map(
        body,
        mesh=fine,
        in_specs=(
            features,
            P("section", "col", ("y", "core")),
            P("section", ("y", "core"), "col"),
            features,
            P("section", "col", ("y", "core")),
        ),
        out_specs=(features, features),
        check_vma=False,
    )
```

```python
import jax
import jax.numpy as jnp
from jax import lax
from jax.experimental import pallas as pl
from jax.experimental.pallas import tpu as pltpu
from jax.sharding import Mesh, PartitionSpec as P

inv_root_two = 0.7071067811865476
inv_root_tau = 0.3989422804014327


def gelu_value(hidden):
    return 0.5 * hidden * (1.0 + lax.erf(hidden * inv_root_two))


def gelu_slope(hidden):
    return (
        0.5 * (1.0 + lax.erf(hidden * inv_root_two))
        + hidden * jnp.exp(-0.5 * hidden * hidden) * inv_root_tau
    )


def product(operand, weight, contract):
    return lax.dot_general(
        operand, weight, (((1,), (contract,)), ((), ())), preferred_element_type=jnp.float32
    )


def swapped(block):
    return lax.ppermute(block, "core", [(0, 1), (1, 0)])


def partial_kernel(chunks_ref, inputs_ref, upstream_ref, up_ref, down_ref, *refs):
    *out_refs, sums_ref = refs
    rows = out_refs[0].shape[1]
    sums_ref[0] = product(inputs_ref[...], up_ref[...], 0).astype(jnp.bfloat16)
    sums_ref[1] = product(upstream_ref[...], down_ref[...], 1).astype(jnp.bfloat16)
    for i, out_ref in enumerate(out_refs):
        start = pl.multiple_of(chunks_ref[i] * rows, rows)
        out_ref[...] = sums_ref[:, pl.ds(start, rows), :]


def partial_sums(chunks, inputs, upstream, w_up, w_down):
    count, width = chunks.shape[0], w_up.shape[1]
    part = (2, inputs.shape[0] // count, width)
    return pl.pallas_call(
        partial_kernel,
        grid_spec=pltpu.PrefetchScalarGridSpec(
            num_scalar_prefetch=1,
            grid=(1,),
            in_specs=[
                pl.BlockSpec(operand.shape, lambda i, chunks: (0, 0))
                for operand in (inputs, upstream, w_up, w_down)
            ],
            out_specs=[pl.BlockSpec(part, lambda i, chunks: (0, 0, 0))] * count,
            scratch_shapes=[pltpu.VMEM((2, inputs.shape[0], width), jnp.bfloat16)],
        ),
        out_shape=[jax.ShapeDtypeStruct(part, jnp.bfloat16)] * count,
        compiler_params=pltpu.CompilerParams(vmem_limit_bytes=58 << 20),
    )(chunks, inputs, upstream, w_up, w_down)


def hidden_kernel(*refs):
    *part_refs, stored_ref, copies_ref = refs
    sums = sum(part_ref[...].astype(jnp.float32) for part_ref in part_refs)
    active = gelu_value(sums[0]).astype(jnp.bfloat16)
    hidden_grad = (sums[1] * gelu_slope(stored_ref[...].astype(jnp.float32))).astype(jnp.bfloat16)
    for i in range(copies_ref.shape[1]):
        copies_ref[0, i] = active
        copies_ref[1, i] = hidden_grad


def hidden_copies(parts, stored, steps=2):
    _, rows, width = parts[0].shape
    tile = rows // steps
    return pl.pallas_call(
        hidden_kernel,
        grid=(steps,),
        in_specs=[pl.BlockSpec((2, tile, width), lambda i: (0, i, 0))] * len(parts)
        + [pl.BlockSpec((tile, width), lambda i: (i, 0))],
        out_specs=pl.BlockSpec((2, len(parts), tile, width), lambda i: (0, 0, i, 0)),
        out_shape=jax.ShapeDtypeStruct((2, len(parts), rows, width), jnp.bfloat16),
        compiler_params=pltpu.CompilerParams(vmem_limit_bytes=63 << 20),
    )(*parts, stored)


def feature_kernel(core_ref, hidden_ref, own_ref, arrived_ref, out_ref):
    def both(first_weight, second_weight, contract):
        total = product(hidden_ref[0], first_weight[...], contract)
        total += product(hidden_ref[1], second_weight[...], contract)
        out_ref[...] = total.astype(jnp.bfloat16)

    @pl.when(core_ref[0] == 0)
    def _():
        both(own_ref, arrived_ref, 0)

    @pl.when(core_ref[0] != 0)
    def _():
        both(arrived_ref, own_ref, 1)


def feature_terms(core, hidden, own, arrived, steps=1):
    _, rows, width = hidden.shape
    tile = rows // steps
    whole = pl.BlockSpec(own.shape, lambda i, core: (0, 0))
    return pl.pallas_call(
        feature_kernel,
        grid_spec=pltpu.PrefetchScalarGridSpec(
            num_scalar_prefetch=1,
            grid=(steps,),
            in_specs=[
                pl.BlockSpec((2, tile, width), lambda i, core: (0, i, 0)),
                whole,
                whole,
            ],
            out_specs=pl.BlockSpec((tile, width), lambda i, core: (i, 0)),
        ),
        out_shape=jax.ShapeDtypeStruct((rows, own.shape[0]), jnp.bfloat16),
        compiler_params=pltpu.CompilerParams(vmem_limit_bytes=32 << 20),
    )(core.reshape(1), hidden, own, arrived)


def body(tokens, up_weight, down_weight, out_grad, saved_hidden):
    inputs, w_up, w_down, upstream = tokens[0], up_weight[0], down_weight[0], out_grad[0]
    ncol, ny, nz = lax.axis_size("col"), lax.axis_size("y"), lax.axis_size("section")
    core = lax.axis_index("core")
    forward = core == 0
    count = inputs.shape[0]
    piece = count // ny
    start = lax.axis_index("y") * piece
    col = lax.axis_index("col")
    reach = sorted(range(1, ncol), key=lambda d: -min(d, ncol - d))
    chunks = jnp.stack([(col + d) % ncol for d in reach] + [col])
    terms = partial_sums(chunks, inputs, upstream, w_up, w_down)
    parts = [terms[-1]] + [
        lax.ppermute(term, "col", [(i, (i + d) % ncol) for i in range(ncol)])
        for d, term in zip(reach, terms)
    ]
    copies = hidden_copies(parts, saved_hidden[0])
    copies = copies.reshape((2 * ncol,) + copies.shape[2:])
    copies, w_up, w_down = lax.optimization_barrier((copies, w_up, w_down))
    own = jnp.where(forward, w_down, w_up)
    arrived = swapped(jnp.where(forward, w_up, w_down))
    residual = jnp.where(
        forward,
        lax.dynamic_slice_in_dim(inputs, start, piece, 0),
        lax.dynamic_slice_in_dim(upstream, start, piece, 0),
    )
    gathered = lax.all_to_all(copies, ("core", "col"), 0, 0, tiled=True)
    chip_sum = feature_terms(core, gathered.reshape(2, count, -1), own, arrived)
    chip_sum, residual = lax.optimization_barrier((chip_sum, residual))
    summed = lax.all_to_all(chip_sum.reshape(ny, piece, -1), "y", 0, 0, tiled=True)
    summed = summed.astype(jnp.float32).sum(0)
    result = (residual.astype(jnp.float32) + summed).astype(jnp.bfloat16)
    route = [(2 * s, 2 * ((s + 1) % nz)) for s in range(nz)]
    route += [(2 * s + 1, 2 * ((s - 1) % nz) + 1) for s in range(nz)]
    moved = lax.ppermute(result, ("section", "core"), route)
    pieces = jnp.broadcast_to(moved[None], (ny,) + moved.shape)
    mine = lax.all_to_all(pieces, "y", 0, 0, tiled=True).reshape(count, -1)
    other = swapped(mine)
    next_tokens = jnp.where(forward, mine, other)
    prev_grads = jnp.where(forward, other, mine)
    return (next_tokens[None], prev_grads[None])


def solution(mesh):
    sections, rows, cols = mesh.devices.shape
    fine = Mesh(mesh.devices.reshape(sections, rows // 2, 2, cols), ("section", "y", "core", "col"))
    features = P("section", None, "col")
    return jax.shard_map(
        body,
        mesh=fine,
        in_specs=(
            features,
            P("section", "col", ("y", "core")),
            P("section", ("y", "core"), "col"),
            features,
            P("section", "col", ("y", "core")),
        ),
        out_specs=(features, features),
        check_vma=False,
    )
```

```python
import jax
import jax.numpy as jnp
from jax import lax
from jax.experimental import pallas as pl
from jax.experimental.pallas import tpu as pltpu
from jax.sharding import Mesh, PartitionSpec as P

inv_root_two = 0.7071067811865476
inv_root_tau = 0.3989422804014327


def gelu_value(hidden):
    return 0.5 * hidden * (1.0 + lax.erf(hidden * inv_root_two))


def gelu_slope(hidden):
    return (
        0.5 * (1.0 + lax.erf(hidden * inv_root_two))
        + hidden * jnp.exp(-0.5 * hidden * hidden) * inv_root_tau
    )


def product(operand, weight, contract):
    return lax.dot_general(
        operand, weight, (((1,), (contract,)), ((), ())), preferred_element_type=jnp.float32
    )


def swapped(block):
    return lax.ppermute(block, "core", [(0, 1), (1, 0)])


def hidden_kernel(parts_ref, stored_ref, copies_ref):
    ncol = parts_ref.shape[0]
    sums = parts_ref[0].astype(jnp.float32)
    for i in range(1, ncol):
        sums += parts_ref[i].astype(jnp.float32)
    active = gelu_value(sums[0]).astype(jnp.bfloat16)
    hidden_grad = (sums[1] * gelu_slope(stored_ref[...].astype(jnp.float32))).astype(jnp.bfloat16)
    for i in range(ncol):
        copies_ref[0, i] = hidden_grad
        copies_ref[1, i] = active


def hidden_copies(parts, stored, steps=2):
    ncol, _, rows, width = parts.shape
    tile = rows // steps
    return pl.pallas_call(
        hidden_kernel,
        grid=(steps,),
        in_specs=[
            pl.BlockSpec((ncol, 2, tile, width), lambda i: (0, 0, i, 0)),
            pl.BlockSpec((tile, width), lambda i: (i, 0)),
        ],
        out_specs=pl.BlockSpec((2, ncol, tile, width), lambda i: (0, 0, i, 0)),
        out_shape=jax.ShapeDtypeStruct((2, ncol, rows, width), jnp.bfloat16),
        compiler_params=pltpu.CompilerParams(vmem_limit_bytes=32 << 20),
    )(parts, stored)


def feature_kernel(core_ref, hidden_ref, own_ref, arrived_ref, out_ref):
    def both(first_weight, second_weight, contract):
        total = product(hidden_ref[0], first_weight[...], contract)
        total += product(hidden_ref[1], second_weight[...], contract)
        out_ref[...] = total.astype(jnp.bfloat16)

    @pl.when(core_ref[0] == 0)
    def _():
        both(own_ref, arrived_ref, 1)

    @pl.when(core_ref[0] != 0)
    def _():
        both(arrived_ref, own_ref, 0)


def feature_terms(core, hidden, own, arrived, steps=1):
    _, rows, width = hidden.shape
    tile = rows // steps
    whole = pl.BlockSpec(own.shape, lambda i, core: (0, 0))
    return pl.pallas_call(
        feature_kernel,
        grid_spec=pltpu.PrefetchScalarGridSpec(
            num_scalar_prefetch=1,
            grid=(steps,),
            in_specs=[
                pl.BlockSpec((2, tile, width), lambda i, core: (0, i, 0)),
                whole,
                whole,
            ],
            out_specs=pl.BlockSpec((tile, width), lambda i, core: (i, 0)),
        ),
        out_shape=jax.ShapeDtypeStruct((rows, own.shape[0]), jnp.bfloat16),
        compiler_params=pltpu.CompilerParams(vmem_limit_bytes=32 << 20),
    )(core.reshape(1), hidden, own, arrived)


def body(tokens, up_weight, down_weight, out_grad, saved_hidden):
    inputs, w_up, w_down, upstream = tokens[0], up_weight[0], down_weight[0], out_grad[0]
    ncol, ny, nz = lax.axis_size("col"), lax.axis_size("y"), lax.axis_size("section")
    core = lax.axis_index("core")
    forward = core == 1
    count = inputs.shape[0]

    def by_col(partial):
        return partial.astype(jnp.bfloat16).reshape(ncol, count // ncol, -1)

    partials = jnp.stack(
        [by_col(product(inputs, w_up, 0)), by_col(product(upstream, w_down, 1))], axis=1
    )
    piece = count // ny
    start = lax.axis_index("y") * piece
    partials, core, forward, start = lax.optimization_barrier((partials, core, forward, start))
    parts = lax.all_to_all(partials, "col", 0, 0, tiled=True)
    own = jnp.where(forward, w_down, w_up)
    arrived = swapped(jnp.where(forward, w_up, w_down))
    copies = hidden_copies(parts, saved_hidden[0])
    copies = copies.reshape((2 * ncol,) + copies.shape[2:])
    gathered = lax.all_to_all(copies, ("core", "col"), 0, 0, tiled=True)
    chip_sum = feature_terms(core, gathered.reshape(2, count, -1), own, arrived)
    residual = jnp.where(
        forward,
        lax.dynamic_slice_in_dim(inputs, start, piece, 0),
        lax.dynamic_slice_in_dim(upstream, start, piece, 0),
    )
    chip_sum, residual = lax.optimization_barrier((chip_sum, residual))
    summed = lax.all_to_all(chip_sum.reshape(ny, piece, -1), "y", 0, 0, tiled=True)
    summed = summed.astype(jnp.float32).sum(0)
    result = (residual.astype(jnp.float32) + summed).astype(jnp.bfloat16)
    route = [(2 * s + 1, 2 * ((s + 1) % nz)) for s in range(nz)]
    route += [(2 * s, 2 * ((s - 1) % nz) + 1) for s in range(nz)]
    moved = lax.ppermute(result, ("section", "core"), route)
    pieces = jnp.broadcast_to(moved[None], (ny,) + moved.shape)
    mine = lax.all_to_all(pieces, "y", 0, 0, tiled=True).reshape(count, -1)
    other = swapped(mine)
    next_tokens = jnp.where(forward, other, mine)
    prev_grads = jnp.where(forward, mine, other)
    return (next_tokens[None], prev_grads[None])


def solution(mesh):
    sections, rows, cols = mesh.devices.shape
    fine = Mesh(mesh.devices.reshape(sections, rows // 2, 2, cols), ("section", "y", "core", "col"))
    features = P("section", None, "col")
    return jax.shard_map(
        body,
        mesh=fine,
        in_specs=(
            features,
            P("section", "col", ("y", "core")),
            P("section", ("y", "core"), "col"),
            features,
            P("section", "col", ("y", "core")),
        ),
        out_specs=(features, features),
        check_vma=False,
    )
```

```python
import jax
import jax.numpy as jnp
from jax import lax
from jax.experimental import pallas as pl
from jax.experimental.pallas import tpu as pltpu
from jax.sharding import Mesh, PartitionSpec as P

inv_root_two = 0.7071067811865476
inv_root_tau = 0.3989422804014327


def gelu_value(hidden):
    return 0.5 * hidden * (1.0 + lax.erf(hidden * inv_root_two))


def gelu_slope(hidden):
    return (
        0.5 * (1.0 + lax.erf(hidden * inv_root_two))
        + hidden * jnp.exp(-0.5 * hidden * hidden) * inv_root_tau
    )


def product(operand, weight, contract):
    return lax.dot_general(
        operand, weight, (((1,), (contract,)), ((), ())), preferred_element_type=jnp.float32
    )


def swapped(block):
    return lax.ppermute(block, "core", [(0, 1), (1, 0)])


def hidden_kernel(*refs):
    *part_refs, stored_ref, copies_ref = refs
    sums = sum(part_ref[...].astype(jnp.float32) for part_ref in part_refs)
    active = gelu_value(sums[0]).astype(jnp.bfloat16)
    hidden_grad = (sums[1] * gelu_slope(stored_ref[...].astype(jnp.float32))).astype(jnp.bfloat16)
    for i in range(copies_ref.shape[1]):
        copies_ref[0, i] = hidden_grad
        copies_ref[1, i] = active


def hidden_copies(parts, stored, steps=2):
    _, rows, width = parts[0].shape
    tile = rows // steps
    return pl.pallas_call(
        hidden_kernel,
        grid=(steps,),
        in_specs=[pl.BlockSpec((2, tile, width), lambda i: (0, i, 0))] * len(parts)
        + [pl.BlockSpec((tile, width), lambda i: (i, 0))],
        out_specs=pl.BlockSpec((2, len(parts), tile, width), lambda i: (0, 0, i, 0)),
        out_shape=jax.ShapeDtypeStruct((2, len(parts), rows, width), jnp.bfloat16),
        compiler_params=pltpu.CompilerParams(vmem_limit_bytes=32 << 20),
    )(*parts, stored)


def feature_kernel(core_ref, hidden_ref, own_ref, arrived_ref, out_ref):
    def both(first_weight, second_weight, contract):
        total = product(hidden_ref[0], first_weight[...], contract)
        total += product(hidden_ref[1], second_weight[...], contract)
        out_ref[...] = total.astype(jnp.bfloat16)

    @pl.when(core_ref[0] == 0)
    def _():
        both(own_ref, arrived_ref, 1)

    @pl.when(core_ref[0] != 0)
    def _():
        both(arrived_ref, own_ref, 0)


def feature_terms(core, hidden, own, arrived, steps=1):
    _, rows, width = hidden.shape
    tile = rows // steps
    whole = pl.BlockSpec(own.shape, lambda i, core: (0, 0))
    return pl.pallas_call(
        feature_kernel,
        grid_spec=pltpu.PrefetchScalarGridSpec(
            num_scalar_prefetch=1,
            grid=(steps,),
            in_specs=[
                pl.BlockSpec((2, tile, width), lambda i, core: (0, i, 0)),
                whole,
                whole,
            ],
            out_specs=pl.BlockSpec((tile, width), lambda i, core: (i, 0)),
        ),
        out_shape=jax.ShapeDtypeStruct((rows, own.shape[0]), jnp.bfloat16),
        compiler_params=pltpu.CompilerParams(vmem_limit_bytes=32 << 20),
    )(core.reshape(1), hidden, own, arrived)


def body(tokens, up_weight, down_weight, out_grad, saved_hidden):
    inputs, w_up, w_down, upstream = tokens[0], up_weight[0], down_weight[0], out_grad[0]
    ncol, ny, nz = lax.axis_size("col"), lax.axis_size("y"), lax.axis_size("section")
    core = lax.axis_index("core")
    forward = core == 1
    count = inputs.shape[0]

    piece = count // ny
    start = lax.axis_index("y") * piece
    partials = [
        product(inputs, w_up, 0).astype(jnp.bfloat16),
        product(upstream, w_down, 1).astype(jnp.bfloat16),
    ]
    col, rows = lax.axis_index("col"), count // ncol

    def chunk_for(distance):
        first = ((col + distance) % ncol) * rows
        return jnp.stack([lax.dynamic_slice_in_dim(p, first, rows, 0) for p in partials])

    parts = [chunk_for(0)]
    for distance in sorted(range(1, ncol), key=lambda d: -min(d, ncol - d)):
        route = [(i, (i + distance) % ncol) for i in range(ncol)]
        parts.append(lax.ppermute(chunk_for(distance), "col", route))
    copies = hidden_copies(parts, saved_hidden[0])
    copies, w_up, w_down = lax.optimization_barrier((copies, w_up, w_down))
    own = jnp.where(forward, w_down, w_up)
    arrived = swapped(jnp.where(forward, w_up, w_down))
    copies = copies.reshape((2 * ncol,) + copies.shape[2:])
    gathered = lax.all_to_all(copies, ("core", "col"), 0, 0, tiled=True)
    chip_sum = feature_terms(core, gathered.reshape(2, count, -1), own, arrived)
    residual = jnp.where(
        forward,
        lax.dynamic_slice_in_dim(inputs, start, piece, 0),
        lax.dynamic_slice_in_dim(upstream, start, piece, 0),
    )
    chip_sum, residual = lax.optimization_barrier((chip_sum, residual))
    summed = lax.all_to_all(chip_sum.reshape(ny, piece, -1), "y", 0, 0, tiled=True)
    summed = summed.astype(jnp.float32).sum(0)
    result = (residual.astype(jnp.float32) + summed).astype(jnp.bfloat16)
    route = [(2 * s + 1, 2 * ((s + 1) % nz)) for s in range(nz)]
    route += [(2 * s, 2 * ((s - 1) % nz) + 1) for s in range(nz)]
    moved = lax.ppermute(result, ("section", "core"), route)
    pieces = jnp.broadcast_to(moved[None], (ny,) + moved.shape)
    mine = lax.all_to_all(pieces, "y", 0, 0, tiled=True).reshape(count, -1)
    other = swapped(mine)
    next_tokens = jnp.where(forward, other, mine)
    prev_grads = jnp.where(forward, mine, other)
    return (next_tokens[None], prev_grads[None])


def solution(mesh):
    sections, rows, cols = mesh.devices.shape
    fine = Mesh(mesh.devices.reshape(sections, rows // 2, 2, cols), ("section", "y", "core", "col"))
    features = P("section", None, "col")
    return jax.shard_map(
        body,
        mesh=fine,
        in_specs=(
            features,
            P("section", "col", ("y", "core")),
            P("section", ("y", "core"), "col"),
            features,
            P("section", "col", ("y", "core")),
        ),
        out_specs=(features, features),
        check_vma=False,
    )
```

```python
import jax
import jax.numpy as jnp
from jax import lax
from jax.experimental import pallas as pl
from jax.experimental.pallas import tpu as pltpu
from jax.sharding import Mesh, PartitionSpec as P

inv_root_two = 0.7071067811865476
inv_root_tau = 0.3989422804014327


def gelu_value(hidden):
    return 0.5 * hidden * (1.0 + lax.erf(hidden * inv_root_two))


def gelu_slope(hidden):
    return (
        0.5 * (1.0 + lax.erf(hidden * inv_root_two))
        + hidden * jnp.exp(-0.5 * hidden * hidden) * inv_root_tau
    )


def product(operand, weight, contract):
    return lax.dot_general(
        operand, weight, (((1,), (contract,)), ((), ())), preferred_element_type=jnp.float32
    )


def swapped(block):
    return lax.ppermute(block, "core", [(0, 1), (1, 0)])


def hidden_kernel(*refs):
    *part_refs, stored_ref, copies_ref = refs
    sums = sum(part_ref[...].astype(jnp.float32) for part_ref in part_refs)
    active = gelu_value(sums[0]).astype(jnp.bfloat16)
    hidden_grad = (sums[1] * gelu_slope(stored_ref[...].astype(jnp.float32))).astype(jnp.bfloat16)
    for i in range(copies_ref.shape[1]):
        copies_ref[0, i] = hidden_grad
        copies_ref[1, i] = active


def hidden_copies(parts, stored, steps=2):
    _, rows, width = parts[0].shape
    tile = rows // steps
    return pl.pallas_call(
        hidden_kernel,
        grid=(steps,),
        in_specs=[pl.BlockSpec((2, tile, width), lambda i: (0, i, 0))] * len(parts)
        + [pl.BlockSpec((tile, width), lambda i: (i, 0))],
        out_specs=pl.BlockSpec((2, len(parts), tile, width), lambda i: (0, 0, i, 0)),
        out_shape=jax.ShapeDtypeStruct((2, len(parts), rows, width), jnp.bfloat16),
        compiler_params=pltpu.CompilerParams(vmem_limit_bytes=32 << 20),
    )(*parts, stored)


def feature_kernel(core_ref, hidden_ref, own_ref, arrived_ref, out_ref):
    def both(first_weight, second_weight, contract):
        total = product(hidden_ref[0], first_weight[...], contract)
        total += product(hidden_ref[1], second_weight[...], contract)
        out_ref[...] = total.astype(jnp.bfloat16)

    @pl.when(core_ref[0] == 0)
    def _():
        both(own_ref, arrived_ref, 1)

    @pl.when(core_ref[0] != 0)
    def _():
        both(arrived_ref, own_ref, 0)


def feature_terms(core, hidden, own, arrived, steps=1):
    _, rows, width = hidden.shape
    tile = rows // steps
    whole = pl.BlockSpec(own.shape, lambda i, core: (0, 0))
    return pl.pallas_call(
        feature_kernel,
        grid_spec=pltpu.PrefetchScalarGridSpec(
            num_scalar_prefetch=1,
            grid=(steps,),
            in_specs=[
                pl.BlockSpec((2, tile, width), lambda i, core: (0, i, 0)),
                whole,
                whole,
            ],
            out_specs=pl.BlockSpec((tile, width), lambda i, core: (i, 0)),
        ),
        out_shape=jax.ShapeDtypeStruct((rows, own.shape[0]), jnp.bfloat16),
        compiler_params=pltpu.CompilerParams(vmem_limit_bytes=32 << 20),
    )(core.reshape(1), hidden, own, arrived)


def body(tokens, up_weight, down_weight, out_grad, saved_hidden):
    inputs, w_up, w_down, upstream = tokens[0], up_weight[0], down_weight[0], out_grad[0]
    ncol, ny, nz = lax.axis_size("col"), lax.axis_size("y"), lax.axis_size("section")
    core = lax.axis_index("core")
    forward = core == 1
    count = inputs.shape[0]

    piece = count // ny
    start = lax.axis_index("y") * piece
    partials = [
        product(inputs, w_up, 0).astype(jnp.bfloat16),
        product(upstream, w_down, 1).astype(jnp.bfloat16),
    ]
    col, rows = lax.axis_index("col"), count // ncol

    def chunk_for(distance):
        first = ((col + distance) % ncol) * rows
        return jnp.stack([lax.dynamic_slice_in_dim(p, first, rows, 0) for p in partials])

    parts = [chunk_for(0)]
    for distance in sorted(range(1, ncol), key=lambda d: min(d, ncol - d)):
        route = [(i, (i + distance) % ncol) for i in range(ncol)]
        parts.append(lax.ppermute(chunk_for(distance), "col", route))
    copies = hidden_copies(parts, saved_hidden[0])
    copies, w_up, w_down = lax.optimization_barrier((copies, w_up, w_down))
    own = jnp.where(forward, w_down, w_up)
    arrived = swapped(jnp.where(forward, w_up, w_down))
    copies = copies.reshape((2 * ncol,) + copies.shape[2:])
    gathered = lax.all_to_all(copies, ("core", "col"), 0, 0, tiled=True)
    chip_sum = feature_terms(core, gathered.reshape(2, count, -1), own, arrived)
    residual = jnp.where(
        forward,
        lax.dynamic_slice_in_dim(inputs, start, piece, 0),
        lax.dynamic_slice_in_dim(upstream, start, piece, 0),
    )
    chip_sum, residual = lax.optimization_barrier((chip_sum, residual))
    summed = lax.all_to_all(chip_sum.reshape(ny, piece, -1), "y", 0, 0, tiled=True)
    summed = summed.astype(jnp.float32).sum(0)
    result = (residual.astype(jnp.float32) + summed).astype(jnp.bfloat16)
    route = [(2 * s + 1, 2 * ((s + 1) % nz)) for s in range(nz)]
    route += [(2 * s, 2 * ((s - 1) % nz) + 1) for s in range(nz)]
    moved = lax.ppermute(result, ("section", "core"), route)
    pieces = jnp.broadcast_to(moved[None], (ny,) + moved.shape)
    mine = lax.all_to_all(pieces, "y", 0, 0, tiled=True).reshape(count, -1)
    other = swapped(mine)
    next_tokens = jnp.where(forward, other, mine)
    prev_grads = jnp.where(forward, mine, other)
    return (next_tokens[None], prev_grads[None])


def solution(mesh):
    sections, rows, cols = mesh.devices.shape
    fine = Mesh(mesh.devices.reshape(sections, rows // 2, 2, cols), ("section", "y", "core", "col"))
    features = P("section", None, "col")
    return jax.shard_map(
        body,
        mesh=fine,
        in_specs=(
            features,
            P("section", "col", ("y", "core")),
            P("section", ("y", "core"), "col"),
            features,
            P("section", "col", ("y", "core")),
        ),
        out_specs=(features, features),
        check_vma=False,
    )
```
